32 devices in a mesh: groups: 2 (over y), dp: 4 (over z), mp: 4 (over x, core).
Axes of the slice: x: 2, y: 2, z: 4, core: 2. Of those that a mesh axis runs over, the one named last changes fastest.
Arguments:
- queries: bfloat16 [4, 192, 8192], P(None, ('groups', 'dp'), 'mp'), parts along dimension 1, may hold values from -120 to 120
- new_keys: bfloat16 [4, 192, 1024], P(None, ('groups', 'dp'), 'mp'), parts along dimension 1, may hold values from -4 to 4
- new_values: bfloat16 [4, 192, 1024], P(None, ('groups', 'dp'), 'mp'), parts along dimension 1, may hold values from -4 to 4
- key_cache: bfloat16 [192, 128, 1024], P(('groups', 'dp'), None, 'mp'), parts along dimension 0, may hold values from -5 to 5
- value_cache: bfloat16 [192, 128, 1024], P(('groups', 'dp'), None, 'mp'), parts along dimension 0, may hold values from -4 to 4
- lengths: int32 [192], P('groups'), parts along dimension 0, may hold values from 8 to 124, as said below
- migrations: int32 [16, 3], P('groups'), parts along dimension 0, may hold values from 0 to 95, as said below
- receive_counts: int32 [8], P('groups'), parts along dimension 0, may hold values from 1 to 3, as said below
Outputs:
- attention: bfloat16 [4, 192, 8192], P(None, ('groups', 'dp'), 'mp'), parts along dimension 1
- landed_keys: bfloat16 [24, 128, 1024], P(('groups', 'dp'), None, 'mp'), parts along dimension 0
- landed_values: bfloat16 [24, 128, 1024], P(('groups', 'dp'), None, 'mp'), parts along dimension 0
The draws below stay inside these ranges and needn't reach their ends.
There are 2 independent parts, one for each index of `groups`. The reference program is written for one: setup_inputs(seed, part) draws one part's arguments, and reference() takes and returns one part's arrays. A program takes and returns all parts, laid end to end along the dimension named above; each array names one. Nothing has to cross between parts.
Inputs may be any that keep to these rules, and one draw needn't show every extreme that they name: `lengths`: rows named in migrations hold 64 to 124 cached positions, all other rows 8 to 32; some row holds exactly 124. `migrations`: entries come in order of source, 2 for every source; an entry's row lies among the source's rows (row // 24 equals source); the 2 destinations of one source differ from each other and from the source; every index of dp receives 2 - 1 to 3 rows, and some receive 3. receive_counts[d] is the number of entries of migrations whose destination is d.
All inputs are finite; a program needn't handle non-finite values.
Results may differ from the reference program's by a relative error of at most 0.0049.
Values may be sent and summed in bfloat16 or wider, within the bound.
A program may use at most 64 MiB of HBM per device.

```python
import jax
import jax.numpy as jnp
from jax import lax

HEADS = 64
KV_HEADS = 8
HEAD_DIM = 128
ROWS_DEV = 24
CAP = 128
STEPS = 4
MIG_DEV = 2
RECV_MAX = 3
ROWS = 96
MOVES = 8
N_DP = 4


def shared_keys(key):
    sample = jax.random.normal(key, (ROWS, CAP, KV_HEADS * HEAD_DIM), jnp.float32)
    return jnp.clip(sample, -4.0, 4.0)


def layout(key):
    first_key, second_key = jax.random.split(key)
    device_count = ROWS // ROWS_DEV
    device_order = jax.random.permutation(first_key, device_count).astype(jnp.int32)
    slot_order = jax.vmap(lambda subkey: jax.random.permutation(subkey, ROWS_DEV))(jax.random.split(second_key, device_count)).astype(jnp.int32)
    return (device_order, slot_order)


def routing(key):
    device_order, slot_order = layout(key)
    device_count = ROWS // ROWS_DEV
    pair_count = jax.random.randint(jax.random.fold_in(key, 5), (), 1, device_count // 2 + 1).astype(jnp.int32)
    position = jnp.argsort(device_order).astype(jnp.int32)
    columns = []
    for offset in range(1, MIG_DEV):
        columns.append(device_order[(position + offset) % device_count])
    paired = device_order[(2 * (position // 2) + MIG_DEV + 1) % device_count]
    shifted = device_order[(position + MIG_DEV) % device_count]
    columns.append(jnp.where(position < 2 * pair_count, paired, shifted))
    destinations = jnp.stack(columns, axis=1).astype(jnp.int32)
    return (destinations, slot_order)


def draw_key_cache(key, part):
    shared = shared_keys(key)
    cache_rows = shared
    return cache_rows.astype(jnp.bfloat16)


def draw_queries(key, part):
    key = jax.random.fold_in(key, 12)
    normal_part = jnp.clip(jax.random.normal(key, (STEPS, ROWS, HEADS * HEAD_DIM), jnp.float32), -4.0, 4.0)
    return normal_part.astype(jnp.bfloat16)


def draw_lengths(key, part):
    device_order, slot_order = layout(key)
    key = jax.random.fold_in(key, 21)
    first_key, second_key = jax.random.split(key)
    device_count = ROWS // ROWS_DEV
    short_len = jax.random.randint(first_key, (device_count, ROWS_DEV), 8, CAP // 4 + 1)
    long_len = jax.random.randint(second_key, (device_count, ROWS_DEV), CAP // 2, CAP - STEPS + 1)
    local_slot = jnp.arange(ROWS_DEV, dtype=jnp.int32)[None, :, None]
    is_long = jnp.any(local_slot == slot_order[:, None, :MIG_DEV], axis=2)
    row_lengths = jnp.where(is_long, long_len, short_len)
    longest = (jnp.arange(device_count, dtype=jnp.int32)[:, None] == 0) & (local_slot[:, :, 0] == slot_order[0:1, 0:1])
    row_lengths = jnp.where(longest, CAP - STEPS, row_lengths)
    return row_lengths.reshape(ROWS).astype(jnp.int32)


def draw_migrations(key, part):
    destinations, slot_order = routing(key)
    device_count = ROWS // ROWS_DEV
    source = jnp.broadcast_to(jnp.arange(device_count, dtype=jnp.int32)[:, None], (device_count, MIG_DEV))
    row_ids = source * ROWS_DEV + slot_order[:, :MIG_DEV]
    table = jnp.stack([row_ids, source, destinations], axis=-1)
    return table.reshape(MOVES, 3).astype(jnp.int32)


def draw_receive_counts(key, part):
    destinations, slot_order = routing(key)
    device_count = ROWS // ROWS_DEV
    device_ids = jnp.arange(device_count, dtype=jnp.int32)
    counts = jnp.sum((destinations.reshape(-1)[None, :] == device_ids[:, None]).astype(jnp.int32), axis=1)
    return counts.astype(jnp.int32)


def levels(rng, dims, pieces, least, high):
    factor_of, own = 1.0, jax.random.fold_in(rng, 6)
    for axis_at, blocks in pieces:
        draws = jnp.exp(jax.random.uniform(jax.random.fold_in(own, axis_at), (blocks,), jnp.float32, least / len(pieces), high / len(pieces)))
        factor_of = factor_of * jnp.repeat(draws, dims[axis_at] // blocks).reshape([-1 if axis == axis_at else 1 for axis in range(len(dims))])
    return factor_of


def normal_values(stream_key, shape, deviation, most, cuts=(), kind=jnp.bfloat16):
    loudness = levels(stream_key, shape, cuts, -0.22, 0.18) if cuts else 1.0
    entries = jax.random.normal(stream_key, shape, jnp.float32) * deviation * loudness
    return jnp.minimum(jnp.maximum(entries, -most), most).astype(kind)


def setup_inputs(seed: int = 0, part: int = 0) -> dict:
    splits = jax.random.split(jax.random.key(seed), 9)
    own_keys = jax.random.split(jax.random.fold_in(splits[8], part), 9)
    return {
        "queries": draw_queries(jax.random.fold_in(jax.random.fold_in(splits[8], part), 71), part),
        "new_keys": normal_values(own_keys[1], (STEPS, ROWS, KV_HEADS * HEAD_DIM), 1.0, 4.0, ((1, 4), (2, 4))),
        "new_values": normal_values(own_keys[2], (STEPS, ROWS, KV_HEADS * HEAD_DIM), 1.0, 4.0, ((1, 4), (2, 4))),
        "key_cache": draw_key_cache(jax.random.fold_in(jax.random.fold_in(splits[8], part), 71), part),
        "value_cache": normal_values(own_keys[4], (ROWS, CAP, KV_HEADS * HEAD_DIM), 1.0, 4.0, ((0, 4), (2, 4))),
        "lengths": draw_lengths(jax.random.fold_in(jax.random.fold_in(splits[8], part), 71), part),
        "migrations": draw_migrations(jax.random.fold_in(jax.random.fold_in(splits[8], part), 71), part),
        "receive_counts": draw_receive_counts(jax.random.fold_in(jax.random.fold_in(splits[8], part), 71), part),
    }


masked_score = -1e30


def extend_cache(cache_rows, fresh, row_lengths):
    positions = jnp.arange(cache_rows.shape[1], dtype=jnp.int32)[None, :, None]
    limits = row_lengths.astype(jnp.int32)[:, None, None]
    result = jnp.where(positions < limits, cache_rows, jnp.zeros((), cache_rows.dtype))
    for offset in range(fresh.shape[0]):
        result = jnp.where(positions == limits + offset, fresh[offset][:, None, :], result)
    return result


def attend_row(packed):
    query_rows, key_rows, value_rows, limit = packed
    per_group = HEADS // KV_HEADS
    query_view = query_rows.astype(jnp.float32).reshape(STEPS, KV_HEADS, per_group, HEAD_DIM)
    key_view = key_rows.astype(jnp.float32).reshape(CAP, KV_HEADS, HEAD_DIM)
    value_view = value_rows.astype(jnp.float32).reshape(CAP, KV_HEADS, HEAD_DIM)
    scores = jnp.einsum("skgd,pkd->kgsp", query_view, key_view) * (HEAD_DIM ** -0.5)
    positions = jnp.arange(CAP, dtype=jnp.int32)[None, :]
    allowed = positions <= limit.astype(jnp.int32) + jnp.arange(STEPS, dtype=jnp.int32)[:, None]
    scores = jnp.where(allowed, scores, masked_score)
    highest = jnp.max(scores, axis=-1, keepdims=True)
    exponent = jnp.exp(scores - highest)
    weights = (exponent / jnp.sum(exponent, axis=-1, keepdims=True)).astype(jnp.bfloat16)
    result = jnp.einsum("kgsp,pkd->skgd", weights.astype(jnp.float32), value_view)
    return result.reshape(STEPS, HEADS * HEAD_DIM).astype(jnp.bfloat16)


def reference(queries, new_keys, new_values, key_cache, value_cache, lengths, migrations, receive_counts):
    extended_keys = extend_cache(key_cache, new_keys, lengths)
    extended_values = extend_cache(value_cache, new_values, lengths)
    per_row = lax.map(attend_row, (jnp.transpose(queries, (1, 0, 2)), extended_keys, extended_values, lengths))
    attention = jnp.transpose(per_row, (1, 0, 2))
    destination = migrations[:, 2].astype(jnp.int32)
    row_ids = migrations[:, 0].astype(jnp.int32)
    entry = jnp.arange(MOVES, dtype=jnp.int32)
    earlier = entry[:, None] > entry[None, :]
    same_dest = destination[:, None] == destination[None, :]
    rank_within = jnp.sum(same_dest & earlier, axis=1).astype(jnp.int32)
    slot_ids = jnp.arange(N_DP * RECV_MAX, dtype=jnp.int32)
    slot_device = slot_ids // RECV_MAX
    slot_turn = slot_ids % RECV_MAX
    matches = (destination[None, :] == slot_device[:, None]) & (rank_within[None, :] == slot_turn[:, None])
    slot_valid = jnp.any(matches, axis=1) & (slot_turn < receive_counts[slot_device])
    source_row = jnp.sum(jnp.where(matches, row_ids[None, :], 0), axis=1).astype(jnp.int32)
    zero_value = jnp.zeros((), jnp.bfloat16)
    landed_keys = jnp.where(slot_valid[:, None, None], extended_keys[source_row], zero_value)
    landed_values = jnp.where(slot_valid[:, None, None], extended_values[source_row], zero_value)
    return attention, landed_keys, landed_values
```

```python
import functools

import jax
import jax.numpy as jnp
from jax import lax
from jax.experimental import pallas as pl
from jax.experimental.pallas import tpu as pltpu
from jax.sharding import PartitionSpec as P

HEAD_DIM = 128
MESH = pl.DeviceIdType.MESH
masked_score = -1e30


def partner(me, n, i):
    if n % 2 or n < 4:
        return lax.rem(me + i + 1, n), lax.rem(me + n - i - 1, n)
    h = n // 2
    half = me // h
    pos = me % h
    if i < h:
        base = (1 - half) * h
        return base + (pos + i) % h, base + (pos + h - i) % h
    step = i - h + 1
    base = half * h
    return base + (pos + step) % h, base + (pos + h - step) % h


def slot_of_source(me, n, src):
    if n % 2 or n < 4:
        return jnp.clip(lax.rem(me - src + n, n) - 1, 0, n - 2)
    h = n // 2
    diff = (me % h + h - src % h) % h
    slot = jnp.where(me // h == src // h, h + diff - 1, diff)
    return jnp.clip(slot, 0, n - 2)


def kernel(
    n, rows, leave, land, steps, cap, width, qwidth,
    len_ref, mig_ref, cnt_ref, q_hbm, nk_hbm, nv_hbm, k_hbm, v_hbm,
    attn_hbm, lk_hbm, lv_hbm,
    q, nk, nv, k, v, nkf, nvf, qf, of, attn, sk, sv, rk, rv, lk, lv,
    in_sem, send_sem, recv_sem, out_sem,
):
    me = lax.axis_index("dp")
    kv_local = width // HEAD_DIM
    heads = qwidth // HEAD_DIM
    per = heads // kv_local
    block = heads * steps

    ins = []
    for i, (src, dst) in enumerate(((nk_hbm, nk), (k_hbm, k), (nv_hbm, nv), (v_hbm, v), (q_hbm, q))):
        copy = pltpu.make_async_copy(src, dst, in_sem.at[i])
        copy.start()
        ins.append(copy)

    barrier = pltpu.get_barrier_semaphore()
    for i in range(n - 1):
        pl.semaphore_signal(
            barrier, inc=1, device_id={"dp": partner(me, n, i)[0]}, device_id_type=MESH
        )

    def find_slot(peer):
        def body(j, carry):
            at = me * leave + j
            return jnp.where(mig_ref[at, 2] == peer, mig_ref[at, 0] - me * rows, carry)

        return jnp.clip(lax.fori_loop(0, leave, body, jnp.int32(0), unroll=leave <= 4), 0, rows - 1)

    slots = [find_slot(partner(me, n, i)[0]) for i in range(n - 1)]
    slot_lengths = [len_ref[me * rows + s] for s in slots]
    positions = lax.broadcasted_iota(jnp.int32, (cap, width), 0)

    def extend(cache, fresh, row, length):
        out = jnp.where(positions < length, cache[row].astype(jnp.float32), 0.0)
        for j in range(steps):
            out = jnp.where(positions == length + j, fresh[pl.ds(j * rows + row, 1), :], out)
        return out.astype(jnp.bfloat16)

    sends = [[], []]

    def push(which, cache, fresh, staged, landing):
        for i in range(n - 1):
            staged[i] = extend(cache, fresh, slots[i], slot_lengths[i])
            copy = pltpu.make_async_remote_copy(
                src_ref=staged.at[i],
                dst_ref=landing.at[i],
                send_sem=send_sem.at[which, i],
                recv_sem=recv_sem.at[which, i],
                device_id={"dp": partner(me, n, i)[0]},
                device_id_type=MESH,
            )
            copy.start()
            sends[which].append(copy)

    ins[0].wait()
    for j in range(steps):
        nkf[j * rows : (j + 1) * rows, :] = nk[j].astype(jnp.float32)
    ins[1].wait()
    pl.semaphore_wait(barrier, n - 1)
    push(0, k, nkf, sk, rk)
    ins[2].wait()
    for j in range(steps):
        nvf[j * rows : (j + 1) * rows, :] = nv[j].astype(jnp.float32)
    ins[3].wait()
    push(1, v, nvf, sv, rv)

    ins[4].wait()
    for s in range(steps):
        for h in range(heads):
            qf[pl.ds(h * steps + s, rows, stride=block), :] = q[
                s, :, h * HEAD_DIM : (h + 1) * HEAD_DIM
            ].astype(jnp.float32)

    span = per * steps
    at = lax.broadcasted_iota(jnp.int32, (span, cap), 1)
    step_of = lax.broadcasted_iota(jnp.int32, (span, cap), 0) % steps
    reach = at - step_of

    def attend(r, carry):
        length = len_ref[me * rows + r]
        ke = extend(k, nkf, r, length)
        ve = extend(v, nvf, r, length)
        for c in range(kv_local):
            cols = slice(c * HEAD_DIM, (c + 1) * HEAD_DIM)
            rowsl = pl.ds(pl.multiple_of(r * block, block) + c * span, span)
            qh = qf[rowsl, :].astype(jnp.bfloat16)
            sc = lax.dot_general(
                qh, ke[:, cols], (((1,), (1,)), ((), ())), preferred_element_type=jnp.float32
            ) * HEAD_DIM ** (-0.5)
            sc = jnp.where(reach <= length, sc, masked_score)
            e = jnp.exp(sc - jnp.max(sc, axis=-1, keepdims=True))
            w = (e / jnp.sum(e, axis=-1, keepdims=True)).astype(jnp.bfloat16)
            of[rowsl, :] = jnp.dot(w, ve[:, cols], preferred_element_type=jnp.float32)
        return carry

    lax.fori_loop(0, rows, attend, 0, unroll=2)
    for s in range(steps):
        for h in range(heads):
            attn[s, :, h * HEAD_DIM : (h + 1) * HEAD_DIM] = of[
                pl.ds(h * steps + s, rows, stride=block), :
            ].astype(jnp.bfloat16)
    out_attn = pltpu.make_async_copy(attn, attn_hbm, out_sem.at[0])
    out_attn.start()

    count = cnt_ref[me]

    def find_source(t):
        def body(m, carry):
            seen, src = carry
            hit = mig_ref[m, 2] == me
            src = jnp.where(hit & (seen == t), m // leave, src)
            return seen + hit.astype(jnp.int32), src

        seen, src = lax.fori_loop(
            0, n * leave, body, (jnp.int32(0), jnp.int32(0)), unroll=n * leave <= 8
        )
        return slot_of_source(me, n, src), (t < seen) & (t < count)

    outs = []
    picks = [find_source(t) for t in range(land)]
    for which, (landing, staged, out) in enumerate(((rk, lk, lk_hbm), (rv, lv, lv_hbm))):
        for copy in sends[which]:
            copy.wait_recv()
        for t, (slot, valid) in enumerate(picks):
            staged[t] = jnp.where(valid, landing[slot].astype(jnp.float32), 0.0).astype(jnp.bfloat16)
        copy = pltpu.make_async_copy(staged, out, out_sem.at[1 + which])
        copy.start()
        outs.append(copy)
    for group in sends:
        for copy in group:
            copy.wait_send()
    out_attn.wait()
    for copy in outs:
        copy.wait()


def on_device(
    queries, new_keys, new_values, key_cache, value_cache, lengths, migrations, receive_counts
):
    n = lax.axis_size("dp")
    rows, cap, width = key_cache.shape
    steps, _, qwidth = queries.shape
    leave = migrations.shape[0] // n
    land = leave + 1
    heads = qwidth // HEAD_DIM
    bf16, f32 = jnp.bfloat16, jnp.float32
    smem = pl.BlockSpec(memory_space=pltpu.SMEM)
    hbm = pl.BlockSpec(memory_space=pl.ANY)
    row_set = (cap, width)
    return pl.pallas_call(
        functools.partial(kernel, n, rows, leave, land, steps, cap, width, qwidth),
        out_shape=(
            jax.ShapeDtypeStruct(queries.shape, bf16),
            jax.ShapeDtypeStruct((land,) + row_set, bf16),
            jax.ShapeDtypeStruct((land,) + row_set, bf16),
        ),
        in_specs=[smem] * 3 + [hbm] * 5,
        out_specs=(hbm, hbm, hbm),
        scratch_shapes=[
            pltpu.VMEM(queries.shape, bf16),
            pltpu.VMEM(new_keys.shape, bf16),
            pltpu.VMEM(new_values.shape, bf16),
            pltpu.VMEM(key_cache.shape, bf16),
            pltpu.VMEM(value_cache.shape, bf16),
            pltpu.VMEM((steps * rows, width), f32),
            pltpu.VMEM((steps * rows, width), f32),
            pltpu.VMEM((rows * heads * steps, HEAD_DIM), f32),
            pltpu.VMEM((rows * heads * steps, HEAD_DIM), f32),
            pltpu.VMEM(queries.shape, bf16),
            pltpu.VMEM((n - 1,) + row_set, bf16),
            pltpu.VMEM((n - 1,) + row_set, bf16),
            pltpu.VMEM((n - 1,) + row_set, bf16),
            pltpu.VMEM((n - 1,) + row_set, bf16),
            pltpu.VMEM((land,) + row_set, bf16),
            pltpu.VMEM((land,) + row_set, bf16),
            pltpu.SemaphoreType.DMA((5,)),
            pltpu.SemaphoreType.DMA((2, n - 1)),
            pltpu.SemaphoreType.DMA((2, n - 1)),
            pltpu.SemaphoreType.DMA((3,)),
        ],
        compiler_params=pltpu.CompilerParams(
            collective_id=0, has_side_effects=True, vmem_limit_bytes=56 * 2**20
        ),
        name="migrate_attend",
    )(
        lengths, migrations, receive_counts, queries, new_keys, new_values, key_cache, value_cache
    )


def solution(mesh):
    placed = (
        P(None, ("groups", "dp"), "mp"),
        P(None, ("groups", "dp"), "mp"),
        P(None, ("groups", "dp"), "mp"),
        P(("groups", "dp"), None, "mp"),
        P(("groups", "dp"), None, "mp"),
        P("groups"),
        P("groups", None),
        P("groups"),
    )
    return jax.shard_map(
        on_device,
        mesh=mesh,
        in_specs=placed,
        out_specs=(
            P(None, ("groups", "dp"), "mp"),
            P(("groups", "dp"), None, "mp"),
            P(("groups", "dp"), None, "mp"),
        ),
        check_vma=False,
    )
```

```python
import functools

import jax
import jax.numpy as jnp
from jax import lax
from jax.experimental import pallas as pl
from jax.experimental.pallas import tpu as pltpu
from jax.sharding import PartitionSpec as P

HEAD_DIM = 128
MESH = pl.DeviceIdType.MESH
masked_score = -1e30
LONGEST_STAYING = 32
GROUP = 8


def partner(me, n, i):
    if n % 2 or n < 4:
        return lax.rem(me + i + 1, n), lax.rem(me + n - i - 1, n)
    h = n // 2
    half = me // h
    pos = me % h
    if i < h:
        base = (1 - half) * h
        return base + (pos + i) % h, base + (pos + h - i) % h
    step = i - h + 1
    base = half * h
    return base + (pos + step) % h, base + (pos + h - step) % h


def slot_of_source(me, n, src):
    if n % 2 or n < 4:
        return jnp.clip(lax.rem(me - src + n, n) - 1, 0, n - 2)
    h = n // 2
    diff = (me % h + h - src % h) % h
    slot = jnp.where(me // h == src // h, h + diff - 1, diff)
    return jnp.clip(slot, 0, n - 2)


def slot_of_target(me, n, dest):
    if n % 2 or n < 4:
        return jnp.clip(lax.rem(dest - me + n, n) - 1, 0, n - 2)
    h = n // 2
    diff = (dest % h + h - me % h) % h
    slot = jnp.where(me // h == dest // h, h + diff - 1, diff)
    return jnp.clip(slot, 0, n - 2)


def kernel(
    n, rows, leave, land, steps, cap, width, qwidth,
    len_hbm, mig_hbm, cnt_hbm, q_hbm, nk_hbm, nv_hbm, k_hbm, v_hbm,
    attn_hbm, lk_hbm, lv_hbm,
    len_ref, mig_ref, cnt_ref,
    q, nk, nv, k, v, nkf, nvf, qf, of, ofl, attn, sk, sv, rk, rv, lk, lv,
    in_sem, send_sem, recv_sem, out_sem,
):
    me = lax.axis_index("dp")
    kv_local = width // HEAD_DIM
    heads = qwidth // HEAD_DIM
    per = heads // kv_local
    block = heads * steps
    window = min(cap, -(-(LONGEST_STAYING + steps) // 16) * 16)

    ins = []
    for i, (src, dst) in enumerate(
        (
            (mig_hbm, mig_ref),
            (len_hbm, len_ref),
            (cnt_hbm, cnt_ref),
            (nk_hbm, nk),
            (k_hbm, k),
            (nv_hbm, nv),
            (v_hbm, v),
            (q_hbm, q),
        )
    ):
        copy = pltpu.make_async_copy(src, dst, in_sem.at[i])
        copy.start()
        ins.append(copy)

    barrier = pltpu.get_barrier_semaphore()
    for i in range(n - 1):
        pl.semaphore_signal(
            barrier, inc=1, device_id={"dp": partner(me, n, i)[0]}, device_id_type=MESH
        )
    for i in range(3):
        ins[i].wait()

    def own_slot(j):
        return jnp.clip(mig_ref[0, me * leave + j] - me * rows, 0, rows - 1)

    def find_slot(peer):
        def body(j, carry):
            return jnp.where(mig_ref[2, me * leave + j] == peer, own_slot(j), carry)

        return lax.fori_loop(0, leave, body, jnp.int32(0), unroll=leave <= 4)

    slots = [find_slot(partner(me, n, i)[0]) for i in range(n - 1)]
    slot_lengths = [len_ref[me * rows + s] for s in slots]

    def extend(cache, fresh, row, length, size):
        positions = lax.broadcasted_iota(jnp.int32, (size, width), 0)
        out = jnp.where(positions < length, cache[row, :size].astype(jnp.float32), 0.0)
        for j in range(steps):
            out = jnp.where(positions == length + j, fresh[pl.ds(j * rows + row, 1), :], out)
        return out.astype(jnp.bfloat16)

    sends = [[], []]

    def push(which, cache, fresh, staged, landing):
        for i in range(n - 1):
            staged[i] = extend(cache, fresh, slots[i], slot_lengths[i], cap)
            copy = pltpu.make_async_remote_copy(
                src_ref=staged.at[i],
                dst_ref=landing.at[i],
                send_sem=send_sem.at[which, i],
                recv_sem=recv_sem.at[which, i],
                device_id={"dp": partner(me, n, i)[0]},
                device_id_type=MESH,
            )
            copy.start()
            sends[which].append(copy)

    ins[3].wait()
    for j in range(steps):
        nkf[j * rows : (j + 1) * rows, :] = nk[j].astype(jnp.float32)
    ins[4].wait()
    pl.semaphore_wait(barrier, n - 1)
    push(0, k, nkf, sk, rk)
    ins[5].wait()
    for j in range(steps):
        nvf[j * rows : (j + 1) * rows, :] = nv[j].astype(jnp.float32)
    ins[6].wait()
    push(1, v, nvf, sv, rv)

    ins[7].wait()
    for s in range(steps):
        for h in range(heads):
            qf[pl.ds(h * steps + s, rows, stride=block), :] = q[
                s, :, h * HEAD_DIM : (h + 1) * HEAD_DIM
            ].astype(jnp.float32)

    span = per * steps

    def attend(entries, size):
        reach = lax.broadcasted_iota(jnp.int32, (span, size), 1) - (
            lax.broadcasted_iota(jnp.int32, (span, size), 0) % steps
        )
        pairs = [(e, c) for e in entries for c in range(kv_local)]
        cols = [slice(c * HEAD_DIM, (c + 1) * HEAD_DIM) for c in range(kv_local)]
        qs = [
            qf[pl.ds(row * block + c * span, span), :].astype(jnp.bfloat16)
            for (row, _, _, _), c in pairs
        ]
        scs = [
            lax.dot_general(
                qh, ke[:, cols[c]], (((1,), (1,)), ((), ())), preferred_element_type=jnp.float32
            ) * HEAD_DIM ** (-0.5)
            for qh, ((_, _, ke, _), c) in zip(qs, pairs)
        ]
        scs = [
            jnp.where(reach <= length, sc, masked_score)
            for sc, ((_, length, _, _), _) in zip(scs, pairs)
        ]
        tops = [jnp.max(sc, axis=-1, keepdims=True) for sc in scs]
        exps = [jnp.exp(sc - top) for sc, top in zip(scs, tops)]
        sums = [jnp.sum(e, axis=-1, keepdims=True) for e in exps]
        ws = [(e / total).astype(jnp.bfloat16) for e, total in zip(exps, sums)]
        return [
            jnp.dot(w, ve[:, cols[c]], preferred_element_type=jnp.float32)
            for w, ((_, _, _, ve), c) in zip(ws, pairs)
        ]

    def attend_leaving(g, carry):
        entries = []
        for d in range(leave_group):
            slot = own_slot(g * leave_group + d)
            at = slot_of_target(me, n, mig_ref[2, me * leave + g * leave_group + d])
            entries.append((slot, len_ref[me * rows + slot], sk[at], sv[at]))
        parts = attend(entries, cap)
        for x, part in enumerate(parts):
            start = (g * leave_group + x // kv_local) * block + x % kv_local * span
            ofl[pl.ds(pl.multiple_of(start, 8), span), :] = part
        return carry

    leave_group = 2 if leave % 2 == 0 else 1
    lax.fori_loop(0, leave // leave_group, attend_leaving, 0)

    def attend_rows(g, carry):
        entries, redone = [], []
        for d in range(group):
            r = g * group + d
            length = len_ref[me * rows + r]
            at = jnp.int32(-1)
            for j in range(leave):
                at = jnp.where(own_slot(j) == r, j, at)
            entries.append(
                (r, length, extend(k, nkf, r, length, window), extend(v, nvf, r, length, window))
            )
            for c in range(kv_local):
                start = jnp.maximum(at, 0) * block + c * span
                redone.append((at >= 0, ofl[pl.ds(start, span), :]))
        parts = attend(entries, window)
        for x, (part, (again, other)) in enumerate(zip(parts, redone)):
            start = (g * group + x // kv_local) * block + x % kv_local * span
            of[pl.ds(pl.multiple_of(start, 8), span), :] = jnp.where(again, other, part)
        return carry

    group = GROUP if rows % GROUP == 0 else 1
    lax.fori_loop(0, rows // group, attend_rows, 0)
    for s in range(steps):
        for h in range(heads):
            attn[s, :, h * HEAD_DIM : (h + 1) * HEAD_DIM] = of[
                pl.ds(h * steps + s, rows, stride=block), :
            ].astype(jnp.bfloat16)
    out_attn = pltpu.make_async_copy(attn, attn_hbm, out_sem.at[0])
    out_attn.start()

    count = cnt_ref[me]

    def find_source(t):
        def body(m, carry):
            seen, src = carry
            hit = mig_ref[2, m] == me
            src = jnp.where(hit & (seen == t), m // leave, src)
            return seen + hit.astype(jnp.int32), src

        seen, src = lax.fori_loop(
            0, n * leave, body, (jnp.int32(0), jnp.int32(0)), unroll=n * leave <= 8
        )
        return slot_of_source(me, n, src), (t < seen) & (t < count)

    outs = []
    picks = [find_source(t) for t in range(land)]
    for which, (landing, staged, out) in enumerate(((rk, lk, lk_hbm), (rv, lv, lv_hbm))):
        for copy in sends[which]:
            copy.wait_recv()
        for t, (slot, valid) in enumerate(picks):
            staged[t] = jnp.where(valid, landing[slot].astype(jnp.float32), 0.0).astype(jnp.bfloat16)
        copy = pltpu.make_async_copy(staged, out, out_sem.at[1 + which])
        copy.start()
        outs.append(copy)
    for group in sends:
        for copy in group:
            copy.wait_send()
    out_attn.wait()
    for copy in outs:
        copy.wait()


def hand_over(*refs):
    count = (len(refs) - 2) // 3
    given, result, held = refs[:count], refs[count : 2 * count], refs[2 * count : 3 * count]
    in_sem, out_sem = refs[3 * count :]
    ins = [pltpu.make_async_copy(given[i], held[i], in_sem.at[i]) for i in range(count)]
    outs = [pltpu.make_async_copy(held[i], result[i], out_sem.at[i]) for i in range(count)]
    for copy in ins:
        copy.start()
    for i in range(count):
        ins[i].wait()
        outs[i].start()
    for copy in outs:
        copy.wait()


def on_device(
    queries, new_keys, new_values, key_cache, value_cache, lengths, migrations, receive_counts
):
    n = lax.axis_size("dp")
    rows, cap, width = key_cache.shape
    steps, _, qwidth = queries.shape
    leave = migrations.shape[0] // n
    land = leave + 1
    heads = qwidth // HEAD_DIM
    bf16, f32 = jnp.bfloat16, jnp.float32
    hbm = pl.BlockSpec(memory_space=pl.ANY)
    row_set = (cap, width)
    results = pl.pallas_call(
        functools.partial(kernel, n, rows, leave, land, steps, cap, width, qwidth),
        out_shape=(
            jax.ShapeDtypeStruct(queries.shape, bf16),
            jax.ShapeDtypeStruct((land,) + row_set, bf16),
            jax.ShapeDtypeStruct((land,) + row_set, bf16),
        ),
        in_specs=[hbm] * 8,
        out_specs=(hbm, hbm, hbm),
        scratch_shapes=[
            pltpu.SMEM(lengths.shape, jnp.int32),
            pltpu.SMEM(migrations.shape[::-1], jnp.int32),
            pltpu.SMEM(receive_counts.shape, jnp.int32),
            pltpu.VMEM(queries.shape, bf16),
            pltpu.VMEM(new_keys.shape, bf16),
            pltpu.VMEM(new_values.shape, bf16),
            pltpu.VMEM(key_cache.shape, bf16),
            pltpu.VMEM(value_cache.shape, bf16),
            pltpu.VMEM((steps * rows, width), f32),
            pltpu.VMEM((steps * rows, width), f32),
            pltpu.VMEM((rows * heads * steps, HEAD_DIM), f32),
            pltpu.VMEM((rows * heads * steps, HEAD_DIM), f32),
            pltpu.VMEM((leave * heads * steps, HEAD_DIM), f32),
            pltpu.VMEM(queries.shape, bf16),
            pltpu.VMEM((n - 1,) + row_set, bf16),
            pltpu.VMEM((n - 1,) + row_set, bf16),
            pltpu.VMEM((n - 1,) + row_set, bf16),
            pltpu.VMEM((n - 1,) + row_set, bf16),
            pltpu.VMEM((land,) + row_set, bf16),
            pltpu.VMEM((land,) + row_set, bf16),
            pltpu.SemaphoreType.DMA((8,)),
            pltpu.SemaphoreType.DMA((2, n - 1)),
            pltpu.SemaphoreType.DMA((2, n - 1)),
            pltpu.SemaphoreType.DMA((3,)),
        ],
        compiler_params=pltpu.CompilerParams(
            collective_id=0, has_side_effects=True, vmem_limit_bytes=56 * 2**20
        ),
        name="migrate_attend",
    )(
        lengths, migrations.T, receive_counts, queries, new_keys, new_values, key_cache, value_cache
    )
    return pl.pallas_call(
        hand_over,
        out_shape=tuple(jax.ShapeDtypeStruct(r.shape, r.dtype) for r in results),
        in_specs=[hbm] * 3,
        out_specs=(hbm,) * 3,
        scratch_shapes=[pltpu.VMEM(r.shape, r.dtype) for r in results]
        + [pltpu.SemaphoreType.DMA((3,))] * 2,
        compiler_params=pltpu.CompilerParams(vmem_limit_bytes=56 * 2**20),
        name="hand_over",
    )(*results)


def solution(mesh):
    placed = (
        P(None, ("groups", "dp"), "mp"),
        P(None, ("groups", "dp"), "mp"),
        P(None, ("groups", "dp"), "mp"),
        P(("groups", "dp"), None, "mp"),
        P(("groups", "dp"), None, "mp"),
        P("groups"),
        P("groups", None),
        P("groups"),
    )
    return jax.shard_map(
        on_device,
        mesh=mesh,
        in_specs=placed,
        out_specs=(
            P(None, ("groups", "dp"), "mp"),
            P(("groups", "dp"), None, "mp"),
            P(("groups", "dp"), None, "mp"),
        ),
        check_vma=False,
    )
```

```python
import functools

import jax
import jax.numpy as jnp
from jax import lax
from jax.experimental import pallas as pl
from jax.experimental.pallas import tpu as pltpu
from jax.sharding import PartitionSpec as P

HEAD_DIM = 128
MESH = pl.DeviceIdType.MESH
masked_score = -1e30
LONGEST_STAYING = 32
GROUP = 8


def partner(me, n, i):
    if n % 2 or n < 4:
        return lax.rem(me + i + 1, n), lax.rem(me + n - i - 1, n)
    h = n // 2
    half = me // h
    pos = me % h
    if i < h:
        base = (1 - half) * h
        return base + (pos + i) % h, base + (pos + h - i) % h
    step = i - h + 1
    base = half * h
    return base + (pos + step) % h, base + (pos + h - step) % h


def slot_of_source(me, n, src):
    if n % 2 or n < 4:
        return jnp.clip(lax.rem(me - src + n, n) - 1, 0, n - 2)
    h = n // 2
    diff = (me % h + h - src % h) % h
    slot = jnp.where(me // h == src // h, h + diff - 1, diff)
    return jnp.clip(slot, 0, n - 2)


def slot_of_target(me, n, dest):
    if n % 2 or n < 4:
        return jnp.clip(lax.rem(dest - me + n, n) - 1, 0, n - 2)
    h = n // 2
    diff = (dest % h + h - me % h) % h
    slot = jnp.where(me // h == dest // h, h + diff - 1, diff)
    return jnp.clip(slot, 0, n - 2)


def kernel(
    n, rows, leave, land, steps, cap, width, qwidth,
    len_hbm, mig_hbm, cnt_hbm, q_hbm, nk_hbm, nv_hbm, k_hbm, v_hbm,
    attn, lk, lv,
    len_ref, mig_ref, cnt_ref,
    q, nk, nv, k, v, nkf, nvf, qf, of, ofl, sk, sv, rk, rv,
    in_sem, send_sem, recv_sem,
):
    me = lax.axis_index("dp")
    kv_local = width // HEAD_DIM
    heads = qwidth // HEAD_DIM
    per = heads // kv_local
    block = heads * steps
    window = min(cap, -(-(LONGEST_STAYING + steps) // 16) * 16)

    ins = []
    for i, (src, dst) in enumerate(
        (
            (mig_hbm, mig_ref),
            (len_hbm, len_ref),
            (cnt_hbm, cnt_ref),
            (nk_hbm, nk),
            (k_hbm, k),
            (nv_hbm, nv),
            (v_hbm, v),
            (q_hbm, q),
        )
    ):
        copy = pltpu.make_async_copy(src, dst, in_sem.at[i])
        if i < 5:
            copy.start()
        ins.append(copy)

    barrier = pltpu.get_barrier_semaphore()
    for i in range(n - 1):
        pl.semaphore_signal(
            barrier, inc=1, device_id={"dp": partner(me, n, i)[0]}, device_id_type=MESH
        )
    for i in range(3):
        ins[i].wait()

    def own_slot(j):
        return jnp.clip(mig_ref[0, me * leave + j] - me * rows, 0, rows - 1)

    def find_slot(peer):
        def body(j, carry):
            return jnp.where(mig_ref[2, me * leave + j] == peer, own_slot(j), carry)

        return lax.fori_loop(0, leave, body, jnp.int32(0), unroll=leave <= 4)

    slots = [find_slot(partner(me, n, i)[0]) for i in range(n - 1)]
    slot_lengths = [len_ref[me * rows + s] for s in slots]

    def extend(cache, fresh, row, length, size):
        positions = lax.broadcasted_iota(jnp.int32, (size, width), 0)
        out = jnp.where(positions < length, cache[row, :size].astype(jnp.float32), 0.0)
        for j in range(steps):
            out = jnp.where(positions == length + j, fresh[pl.ds(j * rows + row, 1), :], out)
        return out.astype(jnp.bfloat16)

    sends = [[], []]

    def push(which, cache, fresh, staged, landing):
        for i in range(n - 1):
            staged[i] = extend(cache, fresh, slots[i], slot_lengths[i], cap)
            copy = pltpu.make_async_remote_copy(
                src_ref=staged.at[i],
                dst_ref=landing.at[i],
                send_sem=send_sem.at[which, i],
                recv_sem=recv_sem.at[which, i],
                device_id={"dp": partner(me, n, i)[0]},
                device_id_type=MESH,
            )
            copy.start()
            sends[which].append(copy)

    ins[3].wait()
    for j in range(steps):
        nkf[j * rows : (j + 1) * rows, :] = nk[j].astype(jnp.float32)
    ins[4].wait()
    for i in range(5, 8):
        ins[i].start()
    pl.semaphore_wait(barrier, n - 1)
    push(0, k, nkf, sk, rk)
    ins[5].wait()
    for j in range(steps):
        nvf[j * rows : (j + 1) * rows, :] = nv[j].astype(jnp.float32)
    ins[6].wait()
    push(1, v, nvf, sv, rv)

    ins[7].wait()
    for s in range(steps):
        for h in range(heads):
            qf[pl.ds(h * steps + s, rows, stride=block), :] = q[
                s, :, h * HEAD_DIM : (h + 1) * HEAD_DIM
            ].astype(jnp.float32)

    span = per * steps

    def attend(entries, size):
        reach = lax.broadcasted_iota(jnp.int32, (span, size), 1) - (
            lax.broadcasted_iota(jnp.int32, (span, size), 0) % steps
        )
        pairs = [(e, c) for e in entries for c in range(kv_local)]
        cols = [slice(c * HEAD_DIM, (c + 1) * HEAD_DIM) for c in range(kv_local)]
        qs = [
            qf[pl.ds(row * block + c * span, span), :].astype(jnp.bfloat16)
            for (row, _, _, _), c in pairs
        ]
        scs = [
            lax.dot_general(
                qh, ke[:, cols[c]], (((1,), (1,)), ((), ())), preferred_element_type=jnp.float32
            ) * HEAD_DIM ** (-0.5)
            for qh, ((_, _, ke, _), c) in zip(qs, pairs)
        ]
        scs = [
            jnp.where(reach <= length, sc, masked_score)
            for sc, ((_, length, _, _), _) in zip(scs, pairs)
        ]
        tops = [jnp.max(sc, axis=-1, keepdims=True) for sc in scs]
        exps = [jnp.exp(sc - top) for sc, top in zip(scs, tops)]
        sums = [jnp.sum(e, axis=-1, keepdims=True) for e in exps]
        ws = [(e / total).astype(jnp.bfloat16) for e, total in zip(exps, sums)]
        return [
            jnp.dot(w, ve[:, cols[c]], preferred_element_type=jnp.float32)
            for w, ((_, _, _, ve), c) in zip(ws, pairs)
        ]

    def attend_leaving(g, carry):
        entries = []
        for d in range(leave_group):
            slot = own_slot(g * leave_group + d)
            at = slot_of_target(me, n, mig_ref[2, me * leave + g * leave_group + d])
            entries.append((slot, len_ref[me * rows + slot], sk[at], sv[at]))
        parts = attend(entries, cap)
        for x, part in enumerate(parts):
            start = (g * leave_group + x // kv_local) * block + x % kv_local * span
            ofl[pl.ds(pl.multiple_of(start, 8), span), :] = part
        return carry

    leave_group = 2 if leave % 2 == 0 else 1
    lax.fori_loop(0, leave // leave_group, attend_leaving, 0)

    def attend_rows(g, carry):
        entries, redone = [], []
        for d in range(group):
            r = g * group + d
            length = len_ref[me * rows + r]
            at = jnp.int32(-1)
            for j in range(leave):
                at = jnp.where(own_slot(j) == r, j, at)
            entries.append(
                (r, length, extend(k, nkf, r, length, window), extend(v, nvf, r, length, window))
            )
            for c in range(kv_local):
                start = jnp.maximum(at, 0) * block + c * span
                redone.append((at >= 0, ofl[pl.ds(start, span), :]))
        parts = attend(entries, window)
        for x, (part, (again, other)) in enumerate(zip(parts, redone)):
            start = (g * group + x // kv_local) * block + x % kv_local * span
            of[pl.ds(pl.multiple_of(start, 8), span), :] = jnp.where(again, other, part)
        return carry

    group = GROUP if rows % GROUP == 0 else 1
    lax.fori_loop(0, rows // group, attend_rows, 0)
    for s in range(steps):
        for h in range(heads):
            attn[s, :, h * HEAD_DIM : (h + 1) * HEAD_DIM] = of[
                pl.ds(h * steps + s, rows, stride=block), :
            ].astype(jnp.bfloat16)

    count = cnt_ref[me]

    def find_source(t):
        def body(m, carry):
            seen, src = carry
            hit = mig_ref[2, m] == me
            src = jnp.where(hit & (seen == t), m // leave, src)
            return seen + hit.astype(jnp.int32), src

        seen, src = lax.fori_loop(
            0, n * leave, body, (jnp.int32(0), jnp.int32(0)), unroll=n * leave <= 8
        )
        return slot_of_source(me, n, src), (t < seen) & (t < count)

    picks = [find_source(t) for t in range(land)]
    for which, (landing, landed) in enumerate(((rk, lk), (rv, lv))):
        for copy in sends[which]:
            copy.wait_recv()
        for t, (slot, valid) in enumerate(picks):
            landed[t] = jnp.where(valid, landing[slot].astype(jnp.float32), 0.0).astype(jnp.bfloat16)
    for group in sends:
        for copy in group:
            copy.wait_send()


def hand_over(*refs):
    count = len(refs) // 2
    copies = [
        pltpu.make_async_copy(refs[i], refs[count + i], refs[-1].at[i]) for i in range(count)
    ]
    for copy in copies:
        copy.start()
    for copy in copies:
        copy.wait()


def on_device(
    queries, new_keys, new_values, key_cache, value_cache, lengths, migrations, receive_counts
):
    n = lax.axis_size("dp")
    rows, cap, width = key_cache.shape
    steps, _, qwidth = queries.shape
    leave = migrations.shape[0] // n
    land = leave + 1
    heads = qwidth // HEAD_DIM
    bf16, f32 = jnp.bfloat16, jnp.float32
    hbm = pl.BlockSpec(memory_space=pl.ANY)
    vmem = pl.BlockSpec(memory_space=pltpu.VMEM)
    row_set = (cap, width)
    results = pl.pallas_call(
        functools.partial(kernel, n, rows, leave, land, steps, cap, width, qwidth),
        out_shape=(
            pltpu.VMEM(queries.shape, bf16),
            pltpu.VMEM((land,) + row_set, bf16),
            pltpu.VMEM((land,) + row_set, bf16),
        ),
        in_specs=[hbm] * 8,
        out_specs=(vmem, vmem, vmem),
        scratch_shapes=[
            pltpu.SMEM(lengths.shape, jnp.int32),
            pltpu.SMEM(migrations.shape[::-1], jnp.int32),
            pltpu.SMEM(receive_counts.shape, jnp.int32),
            pltpu.VMEM(queries.shape, bf16),
            pltpu.VMEM(new_keys.shape, bf16),
            pltpu.VMEM(new_values.shape, bf16),
            pltpu.VMEM(key_cache.shape, bf16),
            pltpu.VMEM(value_cache.shape, bf16),
            pltpu.VMEM((steps * rows, width), f32),
            pltpu.VMEM((steps * rows, width), f32),
            pltpu.VMEM((rows * heads * steps, HEAD_DIM), f32),
            pltpu.VMEM((rows * heads * steps, HEAD_DIM), f32),
            pltpu.VMEM((leave * heads * steps, HEAD_DIM), f32),
            pltpu.VMEM((n - 1,) + row_set, bf16),
            pltpu.VMEM((n - 1,) + row_set, bf16),
            pltpu.VMEM((n - 1,) + row_set, bf16),
            pltpu.VMEM((n - 1,) + row_set, bf16),
            pltpu.SemaphoreType.DMA((8,)),
            pltpu.SemaphoreType.DMA((2, n - 1)),
            pltpu.SemaphoreType.DMA((2, n - 1)),
        ],
        compiler_params=pltpu.CompilerParams(
            collective_id=0, has_side_effects=True, vmem_limit_bytes=60 * 2**20
        ),
        name="migrate_attend",
    )(
        lengths, migrations.T, receive_counts, queries, new_keys, new_values, key_cache, value_cache
    )
    return pl.pallas_call(
        hand_over,
        out_shape=tuple(jax.ShapeDtypeStruct(r.shape, r.dtype) for r in results),
        in_specs=[vmem] * 3,
        out_specs=(hbm,) * 3,
        scratch_shapes=[pltpu.SemaphoreType.DMA((3,))],
        compiler_params=pltpu.CompilerParams(vmem_limit_bytes=32 * 2**20),
        name="hand_over",
    )(*results)


def solution(mesh):
    placed = (
        P(None, ("groups", "dp"), "mp"),
        P(None, ("groups", "dp"), "mp"),
        P(None, ("groups", "dp"), "mp"),
        P(("groups", "dp"), None, "mp"),
        P(("groups", "dp"), None, "mp"),
        P("groups"),
        P("groups", None),
        P("groups"),
    )
    return jax.shard_map(
        on_device,
        mesh=mesh,
        in_specs=placed,
        out_specs=(
            P(None, ("groups", "dp"), "mp"),
            P(("groups", "dp"), None, "mp"),
            P(("groups", "dp"), None, "mp"),
        ),
        check_vma=False,
    )
```

```python
import functools

import jax
import jax.numpy as jnp
from jax import lax
from jax.experimental import pallas as pl
from jax.experimental.pallas import tpu as pltpu
from jax.sharding import PartitionSpec as P

HEAD_DIM = 128
MESH = pl.DeviceIdType.MESH
masked_score = -1e30
LONGEST_STAYING = 32
GROUP = 8


def partner(me, n, i):
    if n % 2 or n < 4:
        return lax.rem(me + i + 1, n), lax.rem(me + n - i - 1, n)
    h = n // 2
    half = me // h
    pos = me % h
    if i < h:
        base = (1 - half) * h
        return base + (pos + i) % h, base + (pos + h - i) % h
    step = i - h + 1
    base = half * h
    return base + (pos + step) % h, base + (pos + h - step) % h


def slot_of_source(me, n, src):
    if n % 2 or n < 4:
        return jnp.clip(lax.rem(me - src + n, n) - 1, 0, n - 2)
    h = n // 2
    diff = (me % h + h - src % h) % h
    slot = jnp.where(me // h == src // h, h + diff - 1, diff)
    return jnp.clip(slot, 0, n - 2)


def slot_of_target(me, n, dest):
    if n % 2 or n < 4:
        return jnp.clip(lax.rem(dest - me + n, n) - 1, 0, n - 2)
    h = n // 2
    diff = (dest % h + h - me % h) % h
    slot = jnp.where(me // h == dest // h, h + diff - 1, diff)
    return jnp.clip(slot, 0, n - 2)


def kernel(
    n, rows, leave, land, steps, cap, width, qwidth,
    len_hbm, mig_hbm, cnt_hbm, q_hbm, nk_hbm, nv_hbm, k_hbm, v_hbm,
    attn, lk, lv,
    len_ref, mig_ref, cnt_ref,
    q, nk, nv, k, v, nkf, nvf, qf, of, ofl, sk, sv, rk, rv,
    in_sem, send_sem, recv_sem, late_sem,
):
    me = lax.axis_index("dp")
    kv_local = width // HEAD_DIM
    heads = qwidth // HEAD_DIM
    per = heads // kv_local
    block = heads * steps
    window = min(cap, -(-(LONGEST_STAYING + steps) // 16) * 16)

    ins = []
    for i, (src, dst) in enumerate(
        (
            (mig_hbm, mig_ref),
            (len_hbm, len_ref),
            (cnt_hbm, cnt_ref),
            (nk_hbm, nk),
            (k_hbm, k),
            (nv_hbm, nv),
            (v_hbm, v),
            (q_hbm, q),
        )
    ):
        copy = pltpu.make_async_copy(src, dst, in_sem.at[i])
        if i < 5:
            copy.start()
        ins.append(copy)

    barrier = pltpu.get_barrier_semaphore()
    last = n - 1
    h = n // 2
    half, pos = me // h, me % h

    @pl.when(me != last)
    def _():
        for i in range(n - 1):
            pl.semaphore_signal(
                barrier, inc=1, device_id={"dp": partner(me, n, i)[0]}, device_id_type=MESH
            )

    for i in range(3):
        ins[i].wait()

    def own_slot(j):
        return jnp.clip(mig_ref[0, me * leave + j] - me * rows, 0, rows - 1)

    def find_slot(peer):
        def body(j, carry):
            return jnp.where(mig_ref[2, me * leave + j] == peer, own_slot(j), carry)

        return lax.fori_loop(0, leave, body, jnp.int32(0), unroll=leave <= 4)

    order = [((1 - half) * h + x, (x - pos + h) % h) for x in range(h)]
    order += [(half * h + (pos + x) % h, h + x - 1) for x in range(1, h)]
    slots = [find_slot(peer) for peer, _ in order]
    slot_lengths = [len_ref[me * rows + s] for s in slots]

    def extend(cache, fresh, row, length, size):
        positions = lax.broadcasted_iota(jnp.int32, (size, width), 0)
        out = jnp.where(positions < length, cache[row, :size].astype(jnp.float32), 0.0)
        for j in range(steps):
            out = jnp.where(positions == length + j, fresh[pl.ds(j * rows + row, 1), :], out)
        return out.astype(jnp.bfloat16)

    sends = [[], []]

    def push(which, cache, fresh, staged, landing, turns):
        for x in turns:
            peer, i = order[x]
            staged[i] = extend(cache, fresh, slots[x], slot_lengths[x], cap)
            copy = pltpu.make_async_remote_copy(
                src_ref=staged.at[i],
                dst_ref=landing.at[i],
                send_sem=send_sem.at[which, i],
                recv_sem=recv_sem.at[which, i],
                device_id={"dp": peer},
                device_id_type=MESH,
            )
            copy.start()
            sends[which].append(copy)

    ins[3].wait()
    for j in range(steps):
        nkf[j * rows : (j + 1) * rows, :] = nk[j].astype(jnp.float32)
    ins[4].wait()
    for i in range(5, 8):
        ins[i].start()
    pl.semaphore_wait(barrier, jnp.where(me == last, n - 1, n - 2))

    @pl.when(me == last)
    def _():
        for i in range(n - 1):
            pl.semaphore_signal(
                late_sem, inc=1, device_id={"dp": partner(me, n, i)[0]}, device_id_type=MESH
            )

    early, final, near = range(h - 1), range(h - 1, h), range(h, n - 1)
    push(0, k, nkf, sk, rk, early)
    ins[5].wait()
    for j in range(steps):
        nvf[j * rows : (j + 1) * rows, :] = nv[j].astype(jnp.float32)
    ins[6].wait()
    push(1, v, nvf, sv, rv, early)

    @pl.when(half == 0)
    def _():
        pl.semaphore_wait(late_sem, 1)

    push(0, k, nkf, sk, rk, final)
    push(1, v, nvf, sv, rv, final)

    @pl.when((half == 1) & (me != last))
    def _():
        pl.semaphore_wait(late_sem, 1)

    push(0, k, nkf, sk, rk, near)
    push(1, v, nvf, sv, rv, near)

    ins[7].wait()
    for s in range(steps):
        for h in range(heads):
            qf[pl.ds(h * steps + s, rows, stride=block), :] = q[
                s, :, h * HEAD_DIM : (h + 1) * HEAD_DIM
            ].astype(jnp.float32)

    span = per * steps

    def attend(entries, size):
        reach = lax.broadcasted_iota(jnp.int32, (span, size), 1) - (
            lax.broadcasted_iota(jnp.int32, (span, size), 0) % steps
        )
        pairs = [(e, c) for e in entries for c in range(kv_local)]
        cols = [slice(c * HEAD_DIM, (c + 1) * HEAD_DIM) for c in range(kv_local)]
        qs = [
            qf[pl.ds(row * block + c * span, span), :].astype(jnp.bfloat16)
            for (row, _, _, _), c in pairs
        ]
        scs = [
            lax.dot_general(
                qh, ke[:, cols[c]], (((1,), (1,)), ((), ())), preferred_element_type=jnp.float32
            ) * HEAD_DIM ** (-0.5)
            for qh, ((_, _, ke, _), c) in zip(qs, pairs)
        ]
        scs = [
            jnp.where(reach <= length, sc, masked_score)
            for sc, ((_, length, _, _), _) in zip(scs, pairs)
        ]
        tops = [jnp.max(sc, axis=-1, keepdims=True) for sc in scs]
        exps = [jnp.exp(sc - top) for sc, top in zip(scs, tops)]
        sums = [jnp.sum(e, axis=-1, keepdims=True) for e in exps]
        ws = [(e / total).astype(jnp.bfloat16) for e, total in zip(exps, sums)]
        return [
            jnp.dot(w, ve[:, cols[c]], preferred_element_type=jnp.float32)
            for w, ((_, _, _, ve), c) in zip(ws, pairs)
        ]

    def attend_leaving(g, carry):
        entries = []
        for d in range(leave_group):
            slot = own_slot(g * leave_group + d)
            at = slot_of_target(me, n, mig_ref[2, me * leave + g * leave_group + d])
            entries.append((slot, len_ref[me * rows + slot], sk[at], sv[at]))
        parts = attend(entries, cap)
        for x, part in enumerate(parts):
            start = (g * leave_group + x // kv_local) * block + x % kv_local * span
            ofl[pl.ds(pl.multiple_of(start, 8), span), :] = part
        return carry

    leave_group = 2 if leave % 2 == 0 else 1
    lax.fori_loop(0, leave // leave_group, attend_leaving, 0)

    def attend_rows(g, carry):
        entries, redone = [], []
        for d in range(group):
            r = g * group + d
            length = len_ref[me * rows + r]
            at = jnp.int32(-1)
            for j in range(leave):
                at = jnp.where(own_slot(j) == r, j, at)
            entries.append(
                (r, length, extend(k, nkf, r, length, window), extend(v, nvf, r, length, window))
            )
            for c in range(kv_local):
                start = jnp.maximum(at, 0) * block + c * span
                redone.append((at >= 0, ofl[pl.ds(start, span), :]))
        parts = attend(entries, window)
        for x, (part, (again, other)) in enumerate(zip(parts, redone)):
            start = (g * group + x // kv_local) * block + x % kv_local * span
            of[pl.ds(pl.multiple_of(start, 8), span), :] = jnp.where(again, other, part)
        return carry

    group = GROUP if rows % GROUP == 0 else 1
    lax.fori_loop(0, rows // group, attend_rows, 0)
    for s in range(steps):
        for h in range(heads):
            attn[s, :, h * HEAD_DIM : (h + 1) * HEAD_DIM] = of[
                pl.ds(h * steps + s, rows, stride=block), :
            ].astype(jnp.bfloat16)

    count = cnt_ref[me]

    def find_source(t):
        def body(m, carry):
            seen, src = carry
            hit = mig_ref[2, m] == me
            src = jnp.where(hit & (seen == t), m // leave, src)
            return seen + hit.astype(jnp.int32), src

        seen, src = lax.fori_loop(
            0, n * leave, body, (jnp.int32(0), jnp.int32(0)), unroll=n * leave <= 8
        )
        return slot_of_source(me, n, src), (t < seen) & (t < count)

    picks = [find_source(t) for t in range(land)]
    for which, (landing, landed) in enumerate(((rk, lk), (rv, lv))):
        for copy in sends[which]:
            copy.wait_recv()
        for t, (slot, valid) in enumerate(picks):
            landed[t] = jnp.where(valid, landing[slot].astype(jnp.float32), 0.0).astype(jnp.bfloat16)
    for group in sends:
        for copy in group:
            copy.wait_send()


def hand_over(*refs):
    count = len(refs) // 2
    copies = [
        pltpu.make_async_copy(refs[i], refs[count + i], refs[-1].at[i]) for i in range(count)
    ]
    for copy in copies:
        copy.start()
    for copy in copies:
        copy.wait()


def on_device(
    queries, new_keys, new_values, key_cache, value_cache, lengths, migrations, receive_counts
):
    n = lax.axis_size("dp")
    rows, cap, width = key_cache.shape
    steps, _, qwidth = queries.shape
    leave = migrations.shape[0] // n
    land = leave + 1
    heads = qwidth // HEAD_DIM
    bf16, f32 = jnp.bfloat16, jnp.float32
    hbm = pl.BlockSpec(memory_space=pl.ANY)
    vmem = pl.BlockSpec(memory_space=pltpu.VMEM)
    row_set = (cap, width)
    results = pl.pallas_call(
        functools.partial(kernel, n, rows, leave, land, steps, cap, width, qwidth),
        out_shape=(
            pltpu.VMEM(queries.shape, bf16),
            pltpu.VMEM((land,) + row_set, bf16),
            pltpu.VMEM((land,) + row_set, bf16),
        ),
        in_specs=[hbm] * 8,
        out_specs=(vmem, vmem, vmem),
        scratch_shapes=[
            pltpu.SMEM(lengths.shape, jnp.int32),
            pltpu.SMEM(migrations.shape[::-1], jnp.int32),
            pltpu.SMEM(receive_counts.shape, jnp.int32),
            pltpu.VMEM(queries.shape, bf16),
            pltpu.VMEM(new_keys.shape, bf16),
            pltpu.VMEM(new_values.shape, bf16),
            pltpu.VMEM(key_cache.shape, bf16),
            pltpu.VMEM(value_cache.shape, bf16),
            pltpu.VMEM((steps * rows, width), f32),
            pltpu.VMEM((steps * rows, width), f32),
            pltpu.VMEM((rows * heads * steps, HEAD_DIM), f32),
            pltpu.VMEM((rows * heads * steps, HEAD_DIM), f32),
            pltpu.VMEM((leave * heads * steps, HEAD_DIM), f32),
            pltpu.VMEM((n - 1,) + row_set, bf16),
            pltpu.VMEM((n - 1,) + row_set, bf16),
            pltpu.VMEM((n - 1,) + row_set, bf16),
            pltpu.VMEM((n - 1,) + row_set, bf16),
            pltpu.SemaphoreType.DMA((8,)),
            pltpu.SemaphoreType.DMA((2, n - 1)),
            pltpu.SemaphoreType.DMA((2, n - 1)),
            pltpu.SemaphoreType.REGULAR,
        ],
        compiler_params=pltpu.CompilerParams(
            collective_id=0, has_side_effects=True, vmem_limit_bytes=60 * 2**20
        ),
        name="migrate_attend",
    )(
        lengths, migrations.T, receive_counts, queries, new_keys, new_values, key_cache, value_cache
    )
    return pl.pallas_call(
        hand_over,
        out_shape=tuple(jax.ShapeDtypeStruct(r.shape, r.dtype) for r in results),
        in_specs=[vmem] * 3,
        out_specs=(hbm,) * 3,
        scratch_shapes=[pltpu.SemaphoreType.DMA((3,))],
        compiler_params=pltpu.CompilerParams(vmem_limit_bytes=32 * 2**20),
        name="hand_over",
    )(*results)


def solution(mesh):
    placed = (
        P(None, ("groups", "dp"), "mp"),
        P(None, ("groups", "dp"), "mp"),
        P(None, ("groups", "dp"), "mp"),
        P(("groups", "dp"), None, "mp"),
        P(("groups", "dp"), None, "mp"),
        P("groups"),
        P("groups", None),
        P("groups"),
    )
    return jax.shard_map(
        on_device,
        mesh=mesh,
        in_specs=placed,
        out_specs=(
            P(None, ("groups", "dp"), "mp"),
            P(("groups", "dp"), None, "mp"),
            P(("groups", "dp"), None, "mp"),
        ),
        check_vma=False,
    )
```
